32 devices in a mesh: rep: 2 (over y), tp: 8 (over z, x), seq: 2 (over core).
Axes of the slice: x: 2, y: 2, z: 4, core: 2. Of those that a mesh axis runs over, the one named last changes fastest.
Arguments:
- gate_preact: bfloat16 [1536, 28672], P(('rep', 'seq'), 'tp'), parts along dimension 0, may hold values from -6 to 6
- up_preact: bfloat16 [1536, 28672], P(('rep', 'seq'), 'tp'), parts along dimension 0, may hold values from -6 to 6
- weight_codes: int32 [28672, 4096], P('tp'), may hold values from 0 to 255
- scale_down: float32 [8192], P('tp'), may hold values from 0.0006 to 0.0024
- grad_output: bfloat16 [1536, 8192], P(('rep', 'seq'), 'tp'), parts along dimension 0, may hold values from -6 to 6
Outputs:
- grad_gate: bfloat16 [1536, 28672], P(('rep', 'seq'), 'tp'), parts along dimension 0
- grad_up: bfloat16 [1536, 28672], P(('rep', 'seq'), 'tp'), parts along dimension 0
- scale_grad: float32 [16384], P(('rep', 'tp', 'seq')), parts along dimension 0
The draws below stay inside these ranges and needn't reach their ends.
There are 2 independent parts, one for each index of `rep`. The reference program is written for one: setup_inputs(seed, part) draws one part's arguments, and reference() takes and returns one part's arrays. A program takes and returns all parts, laid end to end along the dimension named above; an argument that names none is the same for every part. Nothing has to cross between parts.
All inputs are finite; a program needn't handle non-finite values.
Results may differ from the reference program's by a relative error of at most 0.0051.
Values may be sent and summed in bfloat16 or wider, within the bound.
No kernel may reach another device: no remote copies, remote signals or barrier semaphores. Data moves between devices by JAX's collectives and lax.ppermute only.
A program may use at most 576 MiB of HBM per device.

```python
import math
import jax
import jax.numpy as jnp
from jax import lax

D = 8192
FF = 28672
TOKENS = 768
WORDS = 4096
N_TP = 8


def set_ends(drawn, own_key, low, top_value):
    longest = drawn.shape.index(max(drawn.shape))
    spots = []
    for shift in (0, 1):
        where = [jax.random.randint(jax.random.fold_in(own_key, axis), (), 0, length) for axis, length in enumerate(drawn.shape)]
        where[longest] = (where[longest] + shift) % drawn.shape[longest]
        spots.append(tuple(where))
    return drawn.at[spots[0]].set(low).at[spots[1]].set(top_value)


def block_scale(own_key, dims, split, low, top_value):
    gain, own = 1.0, jax.random.fold_in(own_key, 6)
    for position, shards_of in split:
        draws = jnp.exp(jax.random.uniform(jax.random.fold_in(own, position), (shards_of,), jnp.float32, low / len(split), top_value / len(split)))
        gain = gain * jnp.repeat(draws, dims[position] // shards_of).reshape([-1 if axis == position else 1 for axis in range(len(dims))])
    return gain


def noise(own_key, dims, deviation, most, split=(), held_as=jnp.bfloat16):
    drawn = jax.random.normal(own_key, dims, jnp.float32) * deviation
    if len(split) > 0:
        drawn = block_scale(own_key, dims, split, -0.22, 0.18) * drawn
    return jnp.clip(drawn, min=-most, max=most).astype(held_as)


def setup_inputs(seed: int = 0, part: int = 0) -> dict:
    keys = jax.random.split(jax.random.key(seed), 6)
    part_keys = jax.random.split(jax.random.fold_in(keys[5], part), 6)
    return {
        "gate_preact": noise(part_keys[0], (TOKENS, FF), 1.0, 6.0, ((0, 2), (1, 8))),
        "up_preact": noise(part_keys[1], (TOKENS, FF), 1.0, 6.0, ((0, 2), (1, 8))),
        "weight_codes": set_ends(jax.random.randint(keys[2], (FF, WORDS), 0, 256), jax.random.fold_in(keys[2], 1), 0, 255).astype(jnp.int32),
        "scale_down": jnp.clip(jnp.exp(math.log(0.0024) - 1.3862944 * jax.random.uniform(keys[3], (D,), jnp.float32) ** block_scale(keys[3], (D,), ((0, 8),), -0.2, 0.2)), 0.0006, 0.0024),
        "grad_output": noise(part_keys[4], (TOKENS, D), 1.0, 6.0, ((0, 2), (1, 8))),
    }


def unpack(words):
    shifts = 4 * jnp.arange(2, dtype=jnp.int32)
    nibbles = jnp.bitwise_and(jnp.right_shift(words[:, :, None], shifts[None, None, :]), 15)
    return (nibbles.reshape(words.shape[0], words.shape[1] * 2) - 8).astype(jnp.bfloat16)


def reference(gate_preact, up_preact, weight_codes, scale_down, grad_output):
    gate_vals = gate_preact.astype(jnp.float32)
    up_vals = up_preact.astype(jnp.float32)
    sigmoid_gate = jax.nn.sigmoid(gate_vals)
    hidden = (gate_vals * sigmoid_gate * up_vals).astype(jnp.bfloat16)
    scaled_grad = (grad_output.astype(jnp.float32) * scale_down[None, :]).astype(jnp.bfloat16)
    block_rows = FF // N_TP
    code_blocks = weight_codes.reshape(N_TP, block_rows, D // 2)
    hidden_blocks = hidden.reshape(TOKENS, N_TP, block_rows).transpose(1, 0, 2)

    def add_block(running, pieces):
        code_block, hidden_block = pieces
        centered = unpack(code_block)
        grad_block = lax.dot_general(scaled_grad, centered, (((1,), (1,)), ((), ())), preferred_element_type=jnp.float32)
        cross = lax.dot_general(hidden_block, scaled_grad, (((0,), (0,)), ((), ())), preferred_element_type=jnp.float32)
        return running + jnp.sum(centered.astype(jnp.float32) * cross, axis=0), grad_block

    running, grad_blocks = lax.scan(add_block, jnp.zeros((D,), jnp.float32), (code_blocks, hidden_blocks))
    grad_hidden = grad_blocks.transpose(1, 0, 2).reshape(TOKENS, FF)
    grad_gate = (grad_hidden * up_vals * sigmoid_gate * (1.0 + gate_vals * (1.0 - sigmoid_gate))).astype(jnp.bfloat16)
    grad_up = (grad_hidden * gate_vals * sigmoid_gate).astype(jnp.bfloat16)
    return grad_gate, grad_up, running
```

```python
import functools

import jax
import jax.numpy as jnp
from jax import lax
from jax.experimental import pallas as pl
from jax.experimental.pallas import tpu as pltpu
from jax.sharding import PartitionSpec as P

F32 = jnp.float32
BF16 = jnp.bfloat16
MIB = 1 << 20


def sigmoid(v):
    return 0.5 * jnp.tanh(0.5 * v) + 0.5


def nibbles(words):
    low = (jnp.bitwise_and(words, 15) - 8).astype(F32).astype(BF16)
    high = (jnp.right_shift(words, 4) - 8).astype(F32).astype(BF16)
    return jnp.concatenate([low, high], axis=1)


def cost(flops, bytes_accessed):
    return pl.CostEstimate(flops=int(flops), bytes_accessed=int(bytes_accessed), transcendentals=0)


def scale_kernel(grad_ref, scale_ref, out_ref):
    width = grad_ref.shape[1]
    half = width // 2
    scaled = (grad_ref[...].astype(F32) * scale_ref[...]).astype(BF16)
    source = lax.broadcasted_iota(jnp.int32, (256, 256), 0)
    target = lax.broadcasted_iota(jnp.int32, (256, 256), 1)
    wanted = jnp.where(target < 128, 2 * target, 2 * target - 255)
    pick = (source == wanted).astype(F32).astype(BF16)
    for b in range(width // 256):
        sorted_block = jnp.dot(scaled[:, 256 * b:256 * b + 256], pick, preferred_element_type=F32).astype(BF16)
        out_ref[:, 128 * b:128 * b + 128] = sorted_block[:, :128]
        out_ref[:, half + 128 * b:half + 128 * b + 128] = sorted_block[:, 128:]


def scale_call(grad, scale):
    rows, width = grad.shape
    return pl.pallas_call(
        scale_kernel,
        out_shape=jax.ShapeDtypeStruct((rows, width), BF16),
        name="scale",
        cost_estimate=cost(2 * rows * width * 256, 4 * rows * width),
    )(grad, scale.reshape(1, width))


def hidden_kernel(gate_ref, up_ref, out_ref):
    g = gate_ref[...].astype(F32)
    out_ref[...] = (g * sigmoid(g) * up_ref[...].astype(F32)).astype(BF16)


def hidden_call(gate, up):
    rows, units = gate.shape
    spec = pl.BlockSpec((rows, 512), lambda i: (0, i))
    return pl.pallas_call(
        hidden_kernel,
        grid=(units // 512,),
        in_specs=[spec, spec],
        out_specs=spec,
        out_shape=jax.ShapeDtypeStruct((rows, units), BF16),
        name="hidden",
        cost_estimate=cost(16 * rows * units, 6 * rows * units),
    )(gate, up)


def moments_kernel(order_ref, hidden_ref, words_ref, out_ref):
    shard_words = words_ref.shape[1]
    depth = words_ref.shape[0]
    step = pl.program_id(1)
    part = hidden_ref[:, pl.ds(pl.multiple_of(step * depth, depth), depth)]
    total = None
    for k in range(0, depth, 256):
        product = jnp.dot(part[:, k:k + 256], nibbles(words_ref[k:k + 256, :]), preferred_element_type=F32)
        total = product if total is None else total + product

    @pl.when(step == 0)
    def _():
        out_ref[0, 0] = total[:, :shard_words]
        out_ref[0, 1] = total[:, shard_words:]

    @pl.when(step > 0)
    def _():
        out_ref[0, 0] += total[:, :shard_words]
        out_ref[0, 1] += total[:, shard_words:]


def moments_call(order, hidden, words, first, n, shard_words):
    rows, units = hidden.shape
    depth = units // 2
    return pl.pallas_call(
        moments_kernel,
        grid_spec=pltpu.PrefetchScalarGridSpec(
            num_scalar_prefetch=1,
            grid=(n, units // depth),
            in_specs=[
                pl.BlockSpec((rows, units), lambda s, k, o: (0, 0)),
                pl.BlockSpec((depth, shard_words), lambda s, k, o: (k, o[first + s])),
            ],
            out_specs=pl.BlockSpec((1, 2, rows, shard_words), lambda s, k, o: (s, 0, 0, 0)),
        ),
        out_shape=jax.ShapeDtypeStruct((n, 2, rows, shard_words), F32),
        name="moments",
        compiler_params=pltpu.CompilerParams(vmem_limit_bytes=36 * MIB),
        cost_estimate=cost(4 * n * rows * units * shard_words, 4 * n * units * shard_words),
    )(order, hidden, words)


def back_kernel(n, first, order_ref, *refs):
    grads, words, moments = refs[:n], refs[n:2 * n], refs[2 * n:3 * n]
    out_ref, sums_ref = refs[-2:]
    step = pl.program_id(0)
    total = None if first else refs[3 * n][...]
    for s in range(n):
        product = lax.dot_general(
            grads[s][...], nibbles(words[s][...]), (((1,), (1,)), ((), ())), preferred_element_type=F32
        )
        total = product if total is None else total + product
    out_ref[...] = total
    add_sums(step, grads, moments, sums_ref)


def add_sums(step, grads, moments, sums_ref):
    rows = moments[0].shape[2]
    shard_words = moments[0].shape[3]

    @pl.when(step == 0)
    def _():
        sums_ref[...] = jnp.zeros_like(sums_ref)

    @pl.when(step * rows < grads[0].shape[0])
    def _():
        start = pl.ds(pl.multiple_of(step * rows, rows), rows)
        for s in range(len(grads)):
            for k in range(2):
                columns = slice(k * shard_words, (k + 1) * shard_words)
                terms = grads[s][start, columns].astype(F32) * moments[s][0, k]
                sums_ref[s, k:k + 1] += jnp.sum(terms, axis=0, keepdims=True)


def back_call(order, grads, shards, moments, words, total=None):
    n = len(grads)
    rows, width = grads[0].shape
    units = words.shape[0]
    shard_words = width // 2
    block = 512
    steps = units // block
    first = total is None
    sum_rows = 64
    last = rows // sum_rows - 1
    in_specs = [pl.BlockSpec((rows, width), lambda i, o: (0, 0)) for _ in range(n)]
    in_specs += [
        pl.BlockSpec((block, shard_words), functools.partial(lambda s, i, o: (i, o[s]), s)) for s in shards
    ]
    in_specs += [
        pl.BlockSpec(
            (1, 2, sum_rows, shard_words),
            functools.partial(lambda s, i, o: (s, 0, jnp.minimum(i, last), 0), s),
        )
        for _, s in moments
    ]
    operands = [order] + list(grads) + [words] * n + [m for m, _ in moments]
    aliases = {}
    if not first:
        in_specs.append(pl.BlockSpec((rows, block), lambda i, o: (0, i)))
        aliases = {len(operands): 0}
        operands.append(total)
    return pl.pallas_call(
        functools.partial(back_kernel, n, first),
        grid_spec=pltpu.PrefetchScalarGridSpec(
            num_scalar_prefetch=1,
            grid=(steps,),
            in_specs=in_specs,
            out_specs=[
                pl.BlockSpec((rows, block), lambda i, o: (0, i)),
                pl.BlockSpec((n, 2, shard_words), lambda i, o: (0, 0, 0)),
            ],
        ),
        out_shape=[
            jax.ShapeDtypeStruct((rows, units), F32),
            jax.ShapeDtypeStruct((n, 2, shard_words), F32),
        ],
        name="back",
        input_output_aliases=aliases,
        compiler_params=pltpu.CompilerParams(vmem_limit_bytes=40 * MIB),
        cost_estimate=cost(4 * n * rows * units * shard_words, 4 * n * units * shard_words),
    )(*operands)


def sums_kernel(grad_ref, moments_ref, out_ref):
    shard_words = moments_ref.shape[3]
    for k in range(2):
        columns = slice(k * shard_words, (k + 1) * shard_words)
        terms = grad_ref[:, columns].astype(F32) * moments_ref[0, k]
        out_ref[k:k + 1] = jnp.sum(terms, axis=0, keepdims=True)


def sums_call(grad, moments, place):
    rows, width = grad.shape
    return pl.pallas_call(
        sums_kernel,
        grid=(1,),
        in_specs=[
            pl.BlockSpec((rows, width), lambda i: (0, 0)),
            pl.BlockSpec((1, 2, rows, width // 2), lambda i: (place, 0, 0, 0)),
        ],
        out_specs=pl.BlockSpec((2, width // 2), lambda i: (0, 0)),
        out_shape=jax.ShapeDtypeStruct((2, width // 2), F32),
        name="sums",
        cost_estimate=cost(2 * rows * width, 6 * rows * width),
    )(grad, moments)


def tail_kernel(order_ref, grad_ref, words_ref, total_ref, gate_ref, up_ref, gate_out_ref, up_out_ref):
    grad_hidden = total_ref[...] + lax.dot_general(
        grad_ref[...], nibbles(words_ref[...]), (((1,), (1,)), ((), ())), preferred_element_type=F32
    )
    g = gate_ref[...].astype(F32)
    s = sigmoid(g)
    gate_out_ref[...] = (grad_hidden * up_ref[...].astype(F32) * s * (1.0 + g * (1.0 - s))).astype(BF16)
    up_out_ref[...] = (grad_hidden * g * s).astype(BF16)


def tail_call(order, grad, shard, words, total, gate, up):
    rows, width = grad.shape
    units = words.shape[0]
    block = 512
    wide = pl.BlockSpec((rows, block), lambda i, o: (0, i))
    return pl.pallas_call(
        tail_kernel,
        grid_spec=pltpu.PrefetchScalarGridSpec(
            num_scalar_prefetch=1,
            grid=(units // block,),
            in_specs=[
                pl.BlockSpec((rows, width), lambda i, o: (0, 0)),
                pl.BlockSpec((block, width // 2), lambda i, o: (i, o[shard])),
                wide,
                wide,
                wide,
            ],
            out_specs=[wide, wide],
        ),
        out_shape=[jax.ShapeDtypeStruct((rows, units), BF16)] * 2,
        name="tail",
        compiler_params=pltpu.CompilerParams(vmem_limit_bytes=32 * MIB),
        cost_estimate=cost(2 * rows * units * width, 2 * units * width + 12 * rows * units),
    )(order, grad, words, total, gate, up)


def by_ring(ring, gate, up, words, scale, grad):
    tp = 2 * ring
    place = lax.axis_index("tp")
    core = lax.axis_index("seq")
    z, x = place // 2, place % 2
    shard_words = grad.shape[1] // 2

    def shifted(step, flip=0):
        return [(p, 2 * ((p // 2 + step) % ring) + (p + flip) % 2) for p in range(tp)]

    def hop(v):
        return lax.ppermute(v, "tp", shifted(1))

    def across(v):
        return lax.ppermute(v, "tp", shifted(0, 1))

    order = jnp.stack(
        [2 * ((z - k) % ring) + x for k in range(ring)] + [2 * ((z - k) % ring) + 1 - x for k in range(ring)]
    ).astype(jnp.int32)

    own = scale_call(grad, scale)
    line1 = hop(own)
    cross0 = across(own)
    hidden = hidden_call(gate, up)
    m_a = moments_call(order, hidden, words, 0, 4, shard_words)
    line1, cross0, hidden, m_a = lax.optimization_barrier((line1, cross0, hidden, m_a))
    line2 = hop(line1)
    cross1 = across(line1)
    m_b = moments_call(order, hidden, words, 4, 4, shard_words)
    line2, cross1, m_b = lax.optimization_barrier((line2, cross1, m_b))
    line3 = hop(line2)
    cross2 = across(line2)
    total, sums_a = back_call(
        order, [own, line1, cross0, cross1], [0, 1, 4, 5], [(m_a, 0), (m_a, 1), (m_b, 0), (m_b, 1)], words
    )
    line3, cross2, total, sums_a = lax.optimization_barrier((line3, cross2, total, sums_a))
    cross3 = across(line3)
    total, sums_b = back_call(
        order, [line2, line3, cross2], [2, 3, 6], [(m_a, 2), (m_a, 3), (m_b, 2)], words, total
    )

    mine = jnp.concatenate([sums_a, sums_b], axis=0)
    both = mine + lax.ppermute(mine, "seq", [(0, 1), (1, 0)])
    other = across(jnp.stack([both[2], both[3], both[6]]))
    lines = [both[0] + other[0], both[1] + other[1], both[4] + other[2], both[5]]
    channel = lines[0]
    for k in range(1, ring):
        channel = channel + lax.ppermute(lines[k], "tp", shifted(-k))

    late = sums_call(cross3, m_b, 3)
    pairs = shifted(-3, 1)
    for flip in (0, 1):
        channel = channel + lax.ppermute(
            late, ("tp", "seq"), [(2 * a + c, 2 * b + (c + flip) % 2) for a, b in pairs for c in (0, 1)]
        )
    grad_gate, grad_up = tail_call(order, cross3, 7, words, total, gate, up)
    half = shard_words // 2
    kept = lax.dynamic_slice_in_dim(channel, core * half, half, axis=1)
    return grad_gate, grad_up, kept.T.reshape(-1)


def unpack(words):
    shifts = 4 * jnp.arange(2, dtype=jnp.int32)
    codes = jnp.bitwise_and(jnp.right_shift(words[:, :, None], shifts[None, None, :]), 15)
    return (codes.reshape(words.shape[0], words.shape[1] * 2) - 8).astype(BF16)


def by_gather(gate, up, words, scale, grad):
    g = gate.astype(F32)
    u = up.astype(F32)
    s = jax.nn.sigmoid(g)
    hidden = (g * s * u).astype(BF16)
    centered = unpack(words)
    local = (grad.astype(F32) * scale[None, :]).astype(BF16)
    whole = lax.all_gather(local, "tp", axis=1, tiled=True)
    grad_hidden = lax.dot_general(whole, centered, (((1,), (1,)), ((), ())), preferred_element_type=F32)
    moments = jnp.dot(hidden, centered, preferred_element_type=F32)
    sums = jnp.sum(whole.astype(F32) * moments, axis=0)
    grad_gate = (grad_hidden * u * s * (1.0 + g * (1.0 - s))).astype(BF16)
    grad_up = (grad_hidden * g * s).astype(BF16)
    return grad_gate, grad_up, lax.psum_scatter(sums, ("tp", "seq"), scatter_dimension=0, tiled=True)


def solution(mesh):
    tp = mesh.shape["tp"]
    per_device = functools.partial(by_ring, tp // 2) if tp == 8 and mesh.shape["seq"] == 2 else by_gather
    rows = P(("rep", "seq"), "tp")
    return jax.shard_map(
        per_device,
        mesh=mesh,
        in_specs=(rows, rows, P("tp", None), P("tp"), rows),
        out_specs=(rows, rows, P(("rep", "tp", "seq"))),
        check_vma=False,
    )
```

```python
import functools

import jax
import jax.numpy as jnp
from jax import lax
from jax.experimental import pallas as pl
from jax.experimental.pallas import tpu as pltpu
from jax.sharding import PartitionSpec as P

F32 = jnp.float32
BF16 = jnp.bfloat16
VMEM_LIMIT = 48 << 20


def sigmoid(v):
    return 0.5 * jnp.tanh(0.5 * v) + 0.5


def nibbles(words):
    low = (jnp.bitwise_and(words, 15) - 8).astype(F32).astype(BF16)
    high = (jnp.right_shift(words, 4) - 8).astype(F32).astype(BF16)
    return jnp.concatenate([low, high], axis=1)


HELD = pl.BlockSpec(memory_space=pltpu.VMEM)


def cost(flops, bytes_accessed):
    return pl.CostEstimate(flops=int(flops), bytes_accessed=int(bytes_accessed), transcendentals=0)


def scale_kernel(grad_ref, scale_ref, out_ref):
    width = grad_ref.shape[1]
    half = width // 2
    scaled = (grad_ref[...].astype(F32) * scale_ref[...]).astype(BF16)
    source = lax.broadcasted_iota(jnp.int32, (256, 256), 0)
    target = lax.broadcasted_iota(jnp.int32, (256, 256), 1)
    wanted = jnp.where(target < 128, 2 * target, 2 * target - 255)
    pick = (source == wanted).astype(F32).astype(BF16)
    for b in range(width // 256):
        sorted_block = jnp.dot(scaled[:, 256 * b:256 * b + 256], pick, preferred_element_type=F32).astype(BF16)
        out_ref[:, 128 * b:128 * b + 128] = sorted_block[:, :128]
        out_ref[:, half + 128 * b:half + 128 * b + 128] = sorted_block[:, 128:]


def scale_call(grad, scale):
    rows, width = grad.shape
    return pl.pallas_call(
        scale_kernel,
        out_shape=jax.ShapeDtypeStruct((rows, width), BF16),
        name="scale",
        cost_estimate=cost(2 * rows * width * 256, 4 * rows * width),
    )(grad, scale.reshape(1, width))


def hidden_kernel(gate_ref, up_ref, out_ref):
    g = gate_ref[...].astype(F32)
    out_ref[...] = (g * sigmoid(g) * up_ref[...].astype(F32)).astype(BF16)


def hidden_call(gate, up):
    rows, units = gate.shape
    spec = pl.BlockSpec((96, units), lambda i: (i, 0))
    return pl.pallas_call(
        hidden_kernel,
        grid=(rows // 96,),
        in_specs=[spec, spec],
        out_specs=spec,
        out_shape=jax.ShapeDtypeStruct((rows, units), BF16),
        name="hidden",
        compiler_params=pltpu.CompilerParams(vmem_limit_bytes=VMEM_LIMIT),
        cost_estimate=cost(16 * rows * units, 6 * rows * units),
    )(gate, up)


def moments_kernel(n_known, order_ref, hidden_ref, words_ref, *refs):
    grads, out_ref, sums = refs[:n_known], refs[n_known], refs[n_known + 1:]
    total = None
    for k in range(0, hidden_ref.shape[1], BLOCK):
        product = jnp.dot(
            hidden_ref[:, k:k + BLOCK], nibbles(words_ref[k:k + BLOCK, :]), preferred_element_type=F32
        )
        total = product if total is None else total + product
    out_ref[0] = total
    for s in range(n_known):

        @pl.when(pl.program_id(0) == s)
        def _(s=s):
            sums[s][...] = jnp.sum(grads[s][...].astype(F32) * out_ref[0], axis=0, keepdims=True)


def moments_call(order, shards, hidden, words, shard_words, grads):
    rows, units = hidden.shape
    n = len(shards)
    first, second = shards[0], shards[n // 2]

    def place(s, o):
        return 0, o[jnp.where(s < n // 2, first + s, second - n // 2 + s)]

    width = 2 * shard_words
    out = pl.pallas_call(
        functools.partial(moments_kernel, len(grads)),
        grid_spec=pltpu.PrefetchScalarGridSpec(
            num_scalar_prefetch=1,
            grid=(n,),
            in_specs=[
                HELD,
                pl.BlockSpec((units, shard_words), place),
            ]
            + [HELD] * len(grads),
            out_specs=[pl.BlockSpec((1, rows, width), lambda s, o: (s, 0, 0))]
            + [pl.BlockSpec((1, width), lambda s, o: (0, 0))] * len(grads),
        ),
        out_shape=[jax.ShapeDtypeStruct((n, rows, width), F32)]
        + [jax.ShapeDtypeStruct((1, width), F32)] * len(grads),
        name="moments",
        compiler_params=pltpu.CompilerParams(vmem_limit_bytes=VMEM_LIMIT),
        cost_estimate=cost(4 * n * rows * units * shard_words, 4 * n * units * shard_words),
    )(order, hidden, words, *grads)
    return out[0], out[1:]


BLOCK = 512
SUM_ROWS = 64


def sums_kernel(core_ref, *refs):
    grads, moments, known, outs = refs[:2], refs[2:4], refs[4:10], refs[10:]
    late = [
        jnp.sum(g[...].astype(F32) * m[0], axis=0, keepdims=True) for g, m in zip(grads, moments)
    ]
    rows = [ref[...] for ref in known] + late
    quarter = rows[0].shape[1] // 4
    first = core_ref[0] == 0
    for place, row in enumerate(rows):
        low = jnp.concatenate([row[:, :quarter], row[:, 2 * quarter:3 * quarter]], axis=1)
        high = jnp.concatenate([row[:, quarter:2 * quarter], row[:, 3 * quarter:]], axis=1)
        crossed, k = divmod(place, 4)
        outs[2 * crossed][k:k + 1, :] = jnp.where(first, low, high)
        outs[2 * crossed + 1][k:k + 1, :] = jnp.where(first, high, low)


def sums_call(core, moments, places, grads, known):
    rows, width = grads[0].shape
    n = len(places)
    return pl.pallas_call(
        sums_kernel,
        grid_spec=pltpu.PrefetchScalarGridSpec(
            num_scalar_prefetch=1,
            grid=(1,),
            in_specs=[HELD] * n
            + [pl.BlockSpec((1, rows, width), functools.partial(lambda s, i, c: (s, 0, 0), s)) for s in places]
            + [HELD] * len(known),
            out_specs=[pl.BlockSpec((4, width // 2), lambda i, c: (0, 0))] * 4,
        ),
        out_shape=[jax.ShapeDtypeStruct((4, width // 2), F32)] * 4,
        name="sums",
        compiler_params=pltpu.CompilerParams(vmem_limit_bytes=VMEM_LIMIT),
        cost_estimate=cost(2 * n * rows * width, 6 * n * rows * width),
    )(core.reshape(1).astype(jnp.int32), *grads, *([moments] * n), *known)


def product_kernel(n, n_sums, finish, order_ref, *refs):
    grads, words, moments = refs[:n], refs[n:2 * n], refs[2 * n:2 * n + n_sums]
    rest = refs[2 * n + n_sums:]
    sums = rest[len(rest) - n_sums:]
    step = pl.program_id(0)
    total = None
    for grad_ref, word_ref in zip(grads, words):
        product = lax.dot_general(
            grad_ref[...], nibbles(word_ref[...]), (((1,), (1,)), ((), ())), preferred_element_type=F32
        )
        total = product if total is None else total + product
    finish(total, *rest[:len(rest) - n_sums])
    if n_sums == 0:
        return
    rows = moments[0].shape[1]

    @pl.when(step == 0)
    def _():
        for ref in sums:
            ref[...] = jnp.zeros_like(ref)

    @pl.when(step * rows < grads[0].shape[0])
    def _():
        part = pl.ds(pl.multiple_of(step * rows, rows), rows)
        for s in range(n_sums):
            terms = grads[s][part, :].astype(F32) * moments[s][0]
            sums[s][...] += jnp.sum(terms, axis=0, keepdims=True)


def product_call(name, finish, order, words, shards, grads, moments, wide_in, wide_out):
    n = len(shards)
    units = words.shape[0]
    rows, width = grads[0].shape
    last_rows = rows // SUM_ROWS - 1
    wide = pl.BlockSpec((rows, BLOCK), lambda i, o: (0, i))
    vector = pl.BlockSpec((1, width), lambda i, o: (0, 0))
    in_specs = [HELD] * n
    for s in shards:
        in_specs.append(pl.BlockSpec((BLOCK, width // 2), functools.partial(lambda s, i, o: (i, o[s]), s)))
    for _, s in moments:
        place = functools.partial(lambda s, i, o: (s, jnp.minimum(i, last_rows), 0), s)
        in_specs.append(pl.BlockSpec((1, SUM_ROWS, width), place))
    out = pl.pallas_call(
        functools.partial(product_kernel, n, len(moments), finish),
        grid_spec=pltpu.PrefetchScalarGridSpec(
            num_scalar_prefetch=1,
            grid=(units // BLOCK,),
            in_specs=in_specs + [wide] * len(wide_in),
            out_specs=[wide] * len(wide_out) + [vector] * len(moments),
        ),
        out_shape=[jax.ShapeDtypeStruct((rows, units), kind) for kind in wide_out]
        + [jax.ShapeDtypeStruct((1, width), F32)] * len(moments),
        name=name,
        compiler_params=pltpu.CompilerParams(vmem_limit_bytes=VMEM_LIMIT),
        cost_estimate=cost(2 * n * rows * units * width, 2 * n * units * width),
    )(order, *grads, *([words] * n), *[m for m, _ in moments], *wide_in)
    return out[:len(wide_out)], out[len(wide_out):]


def back(product, total_ref):
    total_ref[...] = product


def tail(product, before_ref, gate_ref, up_ref, gate_out_ref, up_out_ref):
    grad_hidden = before_ref[...] + product
    g = gate_ref[...].astype(F32)
    s = sigmoid(g)
    gate_out_ref[...] = (grad_hidden * up_ref[...].astype(F32) * s * (1.0 + g * (1.0 - s))).astype(BF16)
    up_out_ref[...] = (grad_hidden * g * s).astype(BF16)


def by_ring(gate, up, words, scale, grad):
    ring = 4
    place = lax.axis_index("tp")
    core = lax.axis_index("seq")
    z, x = place // 2, place % 2
    shard_words = grad.shape[1] // 2
    together = lax.optimization_barrier

    def shifted(step, flip=0):
        return [(p, 2 * ((p // 2 + step) % ring) + (p + flip) % 2) for p in range(2 * ring)]

    def move(v, step, flip=0):
        return lax.ppermute(v, "tp", shifted(step, flip))

    k = jnp.arange(2 * ring, dtype=jnp.int32)
    order = 2 * ((z + ring - k % ring) % ring) + (x + k // ring) % 2

    own = scale_call(grad, scale)
    line1 = move(own, 1)
    cross0 = move(own, 0, 1)
    hidden = hidden_call(gate, up)
    own, hidden = together((own, hidden))
    line3 = move(own, -1)
    m_later, _ = moments_call(order, [2, 3, 6, 7], hidden, words, shard_words, [])
    line1, cross0, m_later, hidden = together((line1, cross0, m_later, hidden))
    line2 = move(line1, 1)
    cross1 = move(line1, 0, 1)
    m_soon, (s0, s1, c0) = moments_call(order, [0, 1, 4, 5], hidden, words, shard_words, [own, line1, cross0])
    line3, cross1, m_soon = together((line3, cross1, m_soon))
    cross2 = move(cross1, 1)
    cross3 = move(line3, 0, 1)
    (total,), (s2, s3, c1) = product_call(
        "back", back, order, words, [2, 3, 5, 0, 1, 4], [line2, line3, cross1, own, line1, cross0],
        [(m_later, 0), (m_later, 1), (m_soon, 3)], [], [F32],
    )
    lines, lines_other, crossed, crossed_other = sums_call(
        core, m_later, [2, 3], [cross2, cross3], [s0, s1, s2, s3, c0, c1]
    )
    diagonal = [(2 * a + c, 2 * b + 1 - c) for a, b in shifted(0, 1) for c in (0, 1)]
    lines = lines + lax.ppermute(lines_other, "seq", [(0, 1), (1, 0)])
    lines = lines + move(crossed, 0, 1) + lax.ppermute(crossed_other, ("tp", "seq"), diagonal)
    sent = [move(lines[k:k + 1], -k) for k in range(1, ring)]
    (grad_gate, grad_up), _ = product_call(
        "tail", tail, order, words, [6, 7], [cross2, cross3], [], [total, gate, up], [BF16, BF16]
    )
    channel = lines[0:1] + sent[0] + sent[1] + sent[2]
    return grad_gate, grad_up, channel.reshape(2, shard_words // 2).T.reshape(-1)


def unpack(words):
    shifts = 4 * jnp.arange(2, dtype=jnp.int32)
    codes = jnp.bitwise_and(jnp.right_shift(words[:, :, None], shifts[None, None, :]), 15)
    return (codes.reshape(words.shape[0], words.shape[1] * 2) - 8).astype(BF16)


def by_gather(gate, up, words, scale, grad):
    g = gate.astype(F32)
    u = up.astype(F32)
    s = jax.nn.sigmoid(g)
    hidden = (g * s * u).astype(BF16)
    centered = unpack(words)
    local = (grad.astype(F32) * scale[None, :]).astype(BF16)
    whole = lax.all_gather(local, "tp", axis=1, tiled=True)
    grad_hidden = lax.dot_general(whole, centered, (((1,), (1,)), ((), ())), preferred_element_type=F32)
    moments = jnp.dot(hidden, centered, preferred_element_type=F32)
    sums = jnp.sum(whole.astype(F32) * moments, axis=0)
    grad_gate = (grad_hidden * u * s * (1.0 + g * (1.0 - s))).astype(BF16)
    grad_up = (grad_hidden * g * s).astype(BF16)
    return grad_gate, grad_up, lax.psum_scatter(sums, ("tp", "seq"), scatter_dimension=0, tiled=True)


def solution(mesh):
    tp = mesh.shape["tp"]
    per_device = by_ring if tp == 8 and mesh.shape["seq"] == 2 else by_gather
    rows = P(("rep", "seq"), "tp")
    return jax.shard_map(
        per_device,
        mesh=mesh,
        in_specs=(rows, rows, P("tp", None), P("tp"), rows),
        out_specs=(rows, rows, P(("rep", "tp", "seq"))),
        check_vma=False,
    )
```

```python
import functools

import jax
import jax.numpy as jnp
from jax import lax
from jax.experimental import pallas as pl
from jax.experimental.pallas import tpu as pltpu
from jax.sharding import PartitionSpec as P

F32 = jnp.float32
BF16 = jnp.bfloat16
MIB = 1 << 20
VMEM_MIB = {"hidden": 58, "moments": 50, "back": 46, "sums": 12, "tail": 30}


def sigmoid(v):
    return 0.5 * jnp.tanh(0.5 * v) + 0.5


def nibbles(words):
    low = (jnp.bitwise_and(words, 15) - 8).astype(F32).astype(BF16)
    high = (jnp.right_shift(words, 4) - 8).astype(F32).astype(BF16)
    return jnp.concatenate([low, high], axis=1)


HELD = pl.BlockSpec(memory_space=pltpu.VMEM)


def cost(flops, bytes_accessed):
    return pl.CostEstimate(flops=int(flops), bytes_accessed=int(bytes_accessed), transcendentals=0)


def scale_kernel(grad_ref, scale_ref, out_ref):
    width = grad_ref.shape[1]
    half = width // 2
    scaled = (grad_ref[...].astype(F32) * scale_ref[...]).astype(BF16)
    source = lax.broadcasted_iota(jnp.int32, (256, 256), 0)
    target = lax.broadcasted_iota(jnp.int32, (256, 256), 1)
    wanted = jnp.where(target < 128, 2 * target, 2 * target - 255)
    pick = (source == wanted).astype(F32).astype(BF16)
    for b in range(width // 256):
        sorted_block = jnp.dot(scaled[:, 256 * b:256 * b + 256], pick, preferred_element_type=F32).astype(BF16)
        out_ref[:, 128 * b:128 * b + 128] = sorted_block[:, :128]
        out_ref[:, half + 128 * b:half + 128 * b + 128] = sorted_block[:, 128:]


def scale_call(grad, scale):
    rows, width = grad.shape
    return pl.pallas_call(
        scale_kernel,
        out_shape=jax.ShapeDtypeStruct((rows, width), BF16),
        name="scale",
        cost_estimate=cost(2 * rows * width * 256, 4 * rows * width),
    )(grad, scale.reshape(1, width))


def hidden_kernel(gate_ref, up_ref, out_ref):
    g = gate_ref[...].astype(F32)
    out_ref[...] = (g * sigmoid(g) * up_ref[...].astype(F32)).astype(BF16)


def hidden_call(gate, up):
    rows, units = gate.shape
    spec = pl.BlockSpec((96, units), lambda i: (i, 0))
    return pl.pallas_call(
        hidden_kernel,
        grid=(rows // 96,),
        in_specs=[spec, spec],
        out_specs=spec,
        out_shape=jax.ShapeDtypeStruct((rows, units), BF16),
        name="hidden",
        compiler_params=pltpu.CompilerParams(vmem_limit_bytes=VMEM_MIB["hidden"] * MIB),
        cost_estimate=cost(16 * rows * units, 6 * rows * units),
    )(gate, up)


def moments_kernel(order_ref, hidden_ref, words_ref, out_ref):
    total = None
    for k in range(0, hidden_ref.shape[1], BLOCK):
        product = jnp.dot(
            hidden_ref[:, k:k + BLOCK], nibbles(words_ref[k:k + BLOCK, :]), preferred_element_type=F32
        )
        total = product if total is None else total + product
    out_ref[0] = total.astype(BF16)


def moments_call(order, hidden, words, shard_words):
    rows, units = hidden.shape
    n = order.shape[0]
    width = 2 * shard_words
    return pl.pallas_call(
        moments_kernel,
        grid_spec=pltpu.PrefetchScalarGridSpec(
            num_scalar_prefetch=1,
            grid=(n,),
            in_specs=[
                pl.BlockSpec((rows, units), lambda s, o: (0, 0)),
                pl.BlockSpec((units, shard_words), lambda s, o: (0, o[s])),
            ],
            out_specs=pl.BlockSpec((1, rows, width), lambda s, o: (s, 0, 0)),
        ),
        out_shape=jax.ShapeDtypeStruct((n, rows, width), BF16),
        name="moments",
        compiler_params=pltpu.CompilerParams(vmem_limit_bytes=VMEM_MIB["moments"] * MIB),
        cost_estimate=cost(4 * n * rows * units * shard_words, 4 * n * units * shard_words),
    )(order, hidden, words)


BLOCK = 512
SUM_ROWS = 64


def sums_kernel(core_ref, *refs):
    grads, moments, known, outs = refs[:2], refs[2:4], refs[4:10], refs[10:]
    late = [
        jnp.sum(g[...].astype(F32) * m[0].astype(F32), axis=0, keepdims=True) for g, m in zip(grads, moments)
    ]
    rows = [ref[...] for ref in known] + late
    quarter = rows[0].shape[1] // 4
    first = core_ref[0] == 0
    for place, row in enumerate(rows):
        low = jnp.concatenate([row[:, :quarter], row[:, 2 * quarter:3 * quarter]], axis=1)
        high = jnp.concatenate([row[:, quarter:2 * quarter], row[:, 3 * quarter:]], axis=1)
        crossed, k = divmod(place, 4)
        outs[2 * crossed][k:k + 1, :] = jnp.where(first, low, high)
        outs[2 * crossed + 1][k:k + 1, :] = jnp.where(first, high, low)


def sums_call(core, moments, places, grads, known):
    rows, width = grads[0].shape
    n = len(places)
    return pl.pallas_call(
        sums_kernel,
        grid_spec=pltpu.PrefetchScalarGridSpec(
            num_scalar_prefetch=1,
            grid=(1,),
            in_specs=[HELD] * n
            + [pl.BlockSpec((1, rows, width), functools.partial(lambda s, i, c: (s, 0, 0), s)) for s in places]
            + [HELD] * len(known),
            out_specs=[pl.BlockSpec((4, width // 2), lambda i, c: (0, 0))] * 4,
        ),
        out_shape=[jax.ShapeDtypeStruct((4, width // 2), F32)] * 4,
        name="sums",
        compiler_params=pltpu.CompilerParams(vmem_limit_bytes=VMEM_MIB["sums"] * MIB),
        cost_estimate=cost(2 * n * rows * width, 6 * n * rows * width),
    )(core.reshape(1).astype(jnp.int32), *grads, *([moments] * n), *known)


def product_kernel(n, n_sums, finish, order_ref, *refs):
    grads, words, moments = refs[:n], refs[n:2 * n], refs[2 * n:2 * n + n_sums]
    rest = refs[2 * n + n_sums:]
    sums = rest[len(rest) - n_sums:]
    step = pl.program_id(0)
    total = None
    for grad_ref, word_ref in zip(grads, words):
        product = lax.dot_general(
            grad_ref[...], nibbles(word_ref[...]), (((1,), (1,)), ((), ())), preferred_element_type=F32
        )
        total = product if total is None else total + product
    finish(total, *rest[:len(rest) - n_sums])
    if n_sums == 0:
        return
    rows = moments[0].shape[1]

    @pl.when(step == 0)
    def _():
        for ref in sums:
            ref[...] = jnp.zeros_like(ref)

    @pl.when(step * rows < grads[0].shape[0])
    def _():
        part = pl.ds(pl.multiple_of(step * rows, rows), rows)
        for s in range(n_sums):
            terms = grads[s][part, :].astype(F32) * moments[s][0].astype(F32)
            sums[s][...] += jnp.sum(terms, axis=0, keepdims=True)


def product_call(name, finish, order, words, shards, grads, moments, wide_in, wide_out):
    n = len(shards)
    units = words.shape[0]
    rows, width = grads[0].shape
    last_rows = rows // SUM_ROWS - 1
    wide = pl.BlockSpec((rows, BLOCK), lambda i, o: (0, i))
    vector = pl.BlockSpec((1, width), lambda i, o: (0, 0))
    in_specs = [HELD] * n
    for s in shards:
        in_specs.append(pl.BlockSpec((BLOCK, width // 2), functools.partial(lambda s, i, o: (i, o[s]), s)))
    for _, s in moments:
        place = functools.partial(lambda s, i, o: (s, jnp.minimum(i, last_rows), 0), s)
        in_specs.append(pl.BlockSpec((1, SUM_ROWS, width), place))
    out = pl.pallas_call(
        functools.partial(product_kernel, n, len(moments), finish),
        grid_spec=pltpu.PrefetchScalarGridSpec(
            num_scalar_prefetch=1,
            grid=(units // BLOCK,),
            in_specs=in_specs + [wide] * len(wide_in),
            out_specs=[wide] * len(wide_out) + [vector] * len(moments),
        ),
        out_shape=[jax.ShapeDtypeStruct((rows, units), kind) for kind in wide_out]
        + [jax.ShapeDtypeStruct((1, width), F32)] * len(moments),
        name=name,
        compiler_params=pltpu.CompilerParams(vmem_limit_bytes=VMEM_MIB[name] * MIB),
        cost_estimate=cost(2 * n * rows * units * width, 2 * n * units * width),
    )(order, *grads, *([words] * n), *[m for m, _ in moments], *wide_in)
    return out[:len(wide_out)], out[len(wide_out):]


def back(product, total_ref):
    total_ref[...] = product


def back_more(product, before_ref, total_ref):
    total_ref[...] = before_ref[...] + product


def tail(product, before_ref, gate_ref, up_ref, gate_out_ref, up_out_ref):
    grad_hidden = before_ref[...] + product
    g = gate_ref[...].astype(F32)
    s = sigmoid(g)
    gate_out_ref[...] = (grad_hidden * up_ref[...].astype(F32) * s * (1.0 + g * (1.0 - s))).astype(BF16)
    up_out_ref[...] = (grad_hidden * g * s).astype(BF16)


def by_ring(gate, up, words, scale, grad):
    ring = 4
    place = lax.axis_index("tp")
    core = lax.axis_index("seq")
    z, x = place // 2, place % 2
    shard_words = grad.shape[1] // 2
    together = lax.optimization_barrier

    def shifted(step, flip=0):
        return [(p, 2 * ((p // 2 + step) % ring) + (p + flip) % 2) for p in range(2 * ring)]

    def move(v, step, flip=0):
        return lax.ppermute(v, "tp", shifted(step, flip))

    k = jnp.arange(2 * ring, dtype=jnp.int32)
    order = 2 * ((z + ring - k % ring) % ring) + (x + k // ring) % 2

    own = scale_call(grad, scale)
    line1 = move(own, 1)
    cross0 = move(own, 0, 1)
    hidden = hidden_call(gate, up)
    own, hidden = together((own, hidden))
    line3 = move(own, -1)
    moments = moments_call(order, hidden, words, shard_words)
    line1, cross0, line3, moments = together((line1, cross0, line3, moments))
    line2 = move(line1, 1)
    cross1 = move(line1, 0, 1)
    (total,), (s1, s3, c0) = product_call(
        "back", back, order, words, [1, 3, 4], [line1, line3, cross0], [(moments, s) for s in (1, 3, 4)], [], [F32]
    )
    cross1, total = together((cross1, total))
    cross2 = move(cross1, 1)
    cross3 = move(line3, 0, 1)
    (total,), (s0, s2, c1) = product_call(
        "back", back_more, order, words, [0, 2, 5], [own, line2, cross1],
        [(moments, s) for s in (0, 2, 5)], [total], [F32],
    )

    lines, lines_other, crossed, crossed_other = sums_call(
        core, moments, [6, 7], [cross2, cross3], [s0, s1, s2, s3, c0, c1]
    )
    diagonal = [(2 * a + c, 2 * b + 1 - c) for a, b in shifted(0, 1) for c in (0, 1)]
    lines = lines + lax.ppermute(lines_other, "seq", [(0, 1), (1, 0)])
    lines = lines + move(crossed, 0, 1) + lax.ppermute(crossed_other, ("tp", "seq"), diagonal)
    sent = [move(lines[k:k + 1], -k) for k in range(1, ring)]
    (grad_gate, grad_up), _ = product_call(
        "tail", tail, order, words, [6, 7], [cross2, cross3], [], [total, gate, up], [BF16, BF16]
    )
    channel = lines[0:1] + sent[0] + sent[1] + sent[2]
    return grad_gate, grad_up, channel.reshape(2, shard_words // 2).T.reshape(-1)


def unpack(words):
    shifts = 4 * jnp.arange(2, dtype=jnp.int32)
    codes = jnp.bitwise_and(jnp.right_shift(words[:, :, None], shifts[None, None, :]), 15)
    return (codes.reshape(words.shape[0], words.shape[1] * 2) - 8).astype(BF16)


def by_gather(gate, up, words, scale, grad):
    g = gate.astype(F32)
    u = up.astype(F32)
    s = jax.nn.sigmoid(g)
    hidden = (g * s * u).astype(BF16)
    centered = unpack(words)
    local = (grad.astype(F32) * scale[None, :]).astype(BF16)
    whole = lax.all_gather(local, "tp", axis=1, tiled=True)
    grad_hidden = lax.dot_general(whole, centered, (((1,), (1,)), ((), ())), preferred_element_type=F32)
    moments = jnp.dot(hidden, centered, preferred_element_type=F32)
    sums = jnp.sum(whole.astype(F32) * moments, axis=0)
    grad_gate = (grad_hidden * u * s * (1.0 + g * (1.0 - s))).astype(BF16)
    grad_up = (grad_hidden * g * s).astype(BF16)
    return grad_gate, grad_up, lax.psum_scatter(sums, ("tp", "seq"), scatter_dimension=0, tiled=True)


def solution(mesh):
    tp = mesh.shape["tp"]
    per_device = by_ring if tp == 8 and mesh.shape["seq"] == 2 else by_gather
    rows = P(("rep", "seq"), "tp")
    return jax.shard_map(
        per_device,
        mesh=mesh,
        in_specs=(rows, rows, P("tp", None), P("tp"), rows),
        out_specs=(rows, rows, P(("rep", "tp", "seq"))),
        check_vma=False,
    )
```

```python
import functools

import jax
import jax.numpy as jnp
from jax import lax
from jax.experimental import pallas as pl
from jax.experimental.pallas import tpu as pltpu
from jax.sharding import PartitionSpec as P

F32 = jnp.float32
BF16 = jnp.bfloat16
MIB = 1 << 20
VMEM_MIB = {"hidden": 58, "moments": 60, "back": 46, "sums": 12, "tail": 30}


def sigmoid(v):
    return 0.5 * jnp.tanh(0.5 * v) + 0.5


def nibbles(words):
    low = (jnp.bitwise_and(words, 15) - 8).astype(F32).astype(BF16)
    high = (jnp.right_shift(words, 4) - 8).astype(F32).astype(BF16)
    return jnp.concatenate([low, high], axis=1)


HELD = pl.BlockSpec(memory_space=pltpu.VMEM)


def cost(flops, bytes_accessed):
    return pl.CostEstimate(flops=int(flops), bytes_accessed=int(bytes_accessed), transcendentals=0)


def scale_kernel(grad_ref, scale_ref, out_ref):
    width = grad_ref.shape[1]
    half = width // 2
    scaled = (grad_ref[...].astype(F32) * scale_ref[...]).astype(BF16)
    source = lax.broadcasted_iota(jnp.int32, (256, 256), 0)
    target = lax.broadcasted_iota(jnp.int32, (256, 256), 1)
    wanted = jnp.where(target < 128, 2 * target, 2 * target - 255)
    pick = (source == wanted).astype(F32).astype(BF16)
    for b in range(width // 256):
        sorted_block = jnp.dot(scaled[:, 256 * b:256 * b + 256], pick, preferred_element_type=F32).astype(BF16)
        out_ref[:, 128 * b:128 * b + 128] = sorted_block[:, :128]
        out_ref[:, half + 128 * b:half + 128 * b + 128] = sorted_block[:, 128:]


def scale_call(grad, scale):
    rows, width = grad.shape
    return pl.pallas_call(
        scale_kernel,
        out_shape=jax.ShapeDtypeStruct((rows, width), BF16),
        name="scale",
        cost_estimate=cost(2 * rows * width * 256, 4 * rows * width),
    )(grad, scale.reshape(1, width))


def hidden_kernel(gate_ref, up_ref, out_ref):
    g = gate_ref[...].astype(F32)
    out_ref[...] = (g * sigmoid(g) * up_ref[...].astype(F32)).astype(BF16)


def hidden_call(gate, up):
    rows, units = gate.shape
    spec = pl.BlockSpec((64, units), lambda i: (i, 0))
    return pl.pallas_call(
        hidden_kernel,
        grid=(rows // 64,),
        in_specs=[spec, spec],
        out_specs=spec,
        out_shape=jax.ShapeDtypeStruct((rows, units), BF16),
        name="hidden",
        compiler_params=pltpu.CompilerParams(vmem_limit_bytes=VMEM_MIB["hidden"] * MIB),
        cost_estimate=cost(16 * rows * units, 6 * rows * units),
    )(gate, up)


def moments_kernel(order_ref, hidden_ref, words_ref, out_ref):
    total = None
    for k in range(0, hidden_ref.shape[1], BLOCK):
        product = jnp.dot(
            hidden_ref[:, k:k + BLOCK], nibbles(words_ref[k:k + BLOCK, :]), preferred_element_type=F32
        )
        total = product if total is None else total + product
    out_ref[0] = total.astype(BF16)


def moments_call(order, hidden, words, shard_words):
    rows, units = hidden.shape
    n = order.shape[0]
    width = 2 * shard_words
    return pl.pallas_call(
        moments_kernel,
        grid_spec=pltpu.PrefetchScalarGridSpec(
            num_scalar_prefetch=1,
            grid=(n,),
            in_specs=[
                pl.BlockSpec((rows, units), lambda s, o: (0, 0)),
                pl.BlockSpec((units, shard_words), lambda s, o: (0, o[s])),
            ],
            out_specs=pl.BlockSpec((1, rows, width), lambda s, o: (s, 0, 0)),
        ),
        out_shape=jax.ShapeDtypeStruct((n, rows, width), BF16),
        name="moments",
        compiler_params=pltpu.CompilerParams(vmem_limit_bytes=VMEM_MIB["moments"] * MIB),
        cost_estimate=cost(4 * n * rows * units * shard_words, 4 * n * units * shard_words),
    )(order, hidden, words)


BLOCK = 512
SUM_ROWS = 64


def sums_kernel(core_ref, *refs):
    grads, moments, known, outs = refs[:2], refs[2:4], refs[4:10], refs[10:]
    late = [
        jnp.sum(g[...].astype(F32) * m[0].astype(F32), axis=0, keepdims=True) for g, m in zip(grads, moments)
    ]
    rows = [ref[...] for ref in known] + late
    quarter = rows[0].shape[1] // 4
    first = core_ref[0] == 0
    for place, row in enumerate(rows):
        low = jnp.concatenate([row[:, :quarter], row[:, 2 * quarter:3 * quarter]], axis=1)
        high = jnp.concatenate([row[:, quarter:2 * quarter], row[:, 3 * quarter:]], axis=1)
        crossed, k = divmod(place, 4)
        outs[2 * crossed][k:k + 1, :] = jnp.where(first, low, high)
        outs[2 * crossed + 1][k:k + 1, :] = jnp.where(first, high, low)


def sums_call(core, moments, places, grads, known):
    rows, width = grads[0].shape
    n = len(places)
    return pl.pallas_call(
        sums_kernel,
        grid_spec=pltpu.PrefetchScalarGridSpec(
            num_scalar_prefetch=1,
            grid=(1,),
            in_specs=[HELD] * n
            + [pl.BlockSpec((1, rows, width), functools.partial(lambda s, i, c: (s, 0, 0), s)) for s in places]
            + [HELD] * len(known),
            out_specs=[pl.BlockSpec((4, width // 2), lambda i, c: (0, 0))] * 4,
        ),
        out_shape=[jax.ShapeDtypeStruct((4, width // 2), F32)] * 4,
        name="sums",
        compiler_params=pltpu.CompilerParams(vmem_limit_bytes=VMEM_MIB["sums"] * MIB),
        cost_estimate=cost(2 * n * rows * width, 6 * n * rows * width),
    )(core.reshape(1).astype(jnp.int32), *grads, *([moments] * n), *known)


def product_kernel(n, n_sums, finish, order_ref, *refs):
    grads, words, moments = refs[:n], refs[n:2 * n], refs[2 * n:2 * n + n_sums]
    rest = refs[2 * n + n_sums:]
    sums = rest[len(rest) - n_sums:]
    step = pl.program_id(0)
    total = None
    for grad_ref, word_ref in zip(grads, words):
        product = lax.dot_general(
            grad_ref[...], nibbles(word_ref[...]), (((1,), (1,)), ((), ())), preferred_element_type=F32
        )
        total = product if total is None else total + product
    finish(total, *rest[:len(rest) - n_sums])
    if n_sums == 0:
        return
    rows = moments[0].shape[1]

    @pl.when(step == 0)
    def _():
        for ref in sums:
            ref[...] = jnp.zeros_like(ref)

    @pl.when(step * rows < grads[0].shape[0])
    def _():
        part = pl.ds(pl.multiple_of(step * rows, rows), rows)
        for s in range(n_sums):
            terms = grads[s][part, :].astype(F32) * moments[s][0].astype(F32)
            sums[s][...] += jnp.sum(terms, axis=0, keepdims=True)


def product_call(name, finish, order, words, shards, grads, moments, wide_in, wide_out):
    n = len(shards)
    units = words.shape[0]
    rows, width = grads[0].shape
    last_rows = rows // SUM_ROWS - 1
    wide = pl.BlockSpec((rows, BLOCK), lambda i, o: (0, i))
    vector = pl.BlockSpec((1, width), lambda i, o: (0, 0))
    in_specs = [HELD] * n
    for s in shards:
        in_specs.append(pl.BlockSpec((BLOCK, width // 2), functools.partial(lambda s, i, o: (i, o[s]), s)))
    for _, s in moments:
        place = functools.partial(lambda s, i, o: (s, jnp.minimum(i, last_rows), 0), s)
        in_specs.append(pl.BlockSpec((1, SUM_ROWS, width), place))
    out = pl.pallas_call(
        functools.partial(product_kernel, n, len(moments), finish),
        grid_spec=pltpu.PrefetchScalarGridSpec(
            num_scalar_prefetch=1,
            grid=(units // BLOCK,),
            in_specs=in_specs + [wide] * len(wide_in),
            out_specs=[wide] * len(wide_out) + [vector] * len(moments),
        ),
        out_shape=[jax.ShapeDtypeStruct((rows, units), kind) for kind in wide_out]
        + [jax.ShapeDtypeStruct((1, width), F32)] * len(moments),
        name=name,
        compiler_params=pltpu.CompilerParams(vmem_limit_bytes=VMEM_MIB[name] * MIB),
        cost_estimate=cost(2 * n * rows * units * width, 2 * n * units * width),
    )(order, *grads, *([words] * n), *[m for m, _ in moments], *wide_in)
    return out[:len(wide_out)], out[len(wide_out):]


def back(product, total_ref):
    total_ref[...] = product


def back_more(product, before_ref, total_ref):
    total_ref[...] = before_ref[...] + product


def tail(product, before_ref, gate_ref, up_ref, gate_out_ref, up_out_ref):
    grad_hidden = before_ref[...] + product
    g = gate_ref[...].astype(F32)
    s = sigmoid(g)
    gate_out_ref[...] = (grad_hidden * up_ref[...].astype(F32) * s * (1.0 + g * (1.0 - s))).astype(BF16)
    up_out_ref[...] = (grad_hidden * g * s).astype(BF16)


def by_ring(gate, up, words, scale, grad):
    ring = 4
    place = lax.axis_index("tp")
    core = lax.axis_index("seq")
    z, x = place // 2, place % 2
    shard_words = grad.shape[1] // 2
    together = lax.optimization_barrier

    def shifted(step, flip=0):
        return [(p, 2 * ((p // 2 + step) % ring) + (p + flip) % 2) for p in range(2 * ring)]

    def move(v, step, flip=0):
        return lax.ppermute(v, "tp", shifted(step, flip))

    k = jnp.arange(2 * ring, dtype=jnp.int32)
    order = 2 * ((z + ring - k % ring) % ring) + (x + k // ring) % 2

    own = scale_call(grad, scale)
    line1 = move(own, 1)
    cross0 = move(own, 0, 1)
    hidden = hidden_call(gate, up)
    own, hidden = together((own, hidden))
    line3 = move(own, -1)
    moments = moments_call(order, hidden, words, shard_words)
    line1, cross0, line3, moments = together((line1, cross0, line3, moments))
    line2 = move(line1, 1)
    cross1 = move(line1, 0, 1)
    (total,), (s1, s3, c0) = product_call(
        "back", back, order, words, [1, 3, 4], [line1, line3, cross0], [(moments, s) for s in (1, 3, 4)], [], [F32]
    )
    cross1, total = together((cross1, total))
    cross2 = move(cross1, 1)
    cross3 = move(line3, 0, 1)
    (total,), (s0, s2, c1) = product_call(
        "back", back_more, order, words, [0, 2, 5], [own, line2, cross1],
        [(moments, s) for s in (0, 2, 5)], [total], [F32],
    )

    lines, lines_other, crossed, crossed_other = sums_call(
        core, moments, [6, 7], [cross2, cross3], [s0, s1, s2, s3, c0, c1]
    )
    diagonal = [(2 * a + c, 2 * b + 1 - c) for a, b in shifted(0, 1) for c in (0, 1)]
    lines = lines + lax.ppermute(lines_other, "seq", [(0, 1), (1, 0)])
    lines = lines + move(crossed, 0, 1) + lax.ppermute(crossed_other, ("tp", "seq"), diagonal)
    sent = [move(lines[k:k + 1], -k) for k in range(1, ring)]
    (grad_gate, grad_up), _ = product_call(
        "tail", tail, order, words, [6, 7], [cross2, cross3], [], [total, gate, up], [BF16, BF16]
    )
    channel = lines[0:1] + sent[0] + sent[1] + sent[2]
    return grad_gate, grad_up, channel.reshape(2, shard_words // 2).T.reshape(-1)


def unpack(words):
    shifts = 4 * jnp.arange(2, dtype=jnp.int32)
    codes = jnp.bitwise_and(jnp.right_shift(words[:, :, None], shifts[None, None, :]), 15)
    return (codes.reshape(words.shape[0], words.shape[1] * 2) - 8).astype(BF16)


def by_gather(gate, up, words, scale, grad):
    g = gate.astype(F32)
    u = up.astype(F32)
    s = jax.nn.sigmoid(g)
    hidden = (g * s * u).astype(BF16)
    centered = unpack(words)
    local = (grad.astype(F32) * scale[None, :]).astype(BF16)
    whole = lax.all_gather(local, "tp", axis=1, tiled=True)
    grad_hidden = lax.dot_general(whole, centered, (((1,), (1,)), ((), ())), preferred_element_type=F32)
    moments = jnp.dot(hidden, centered, preferred_element_type=F32)
    sums = jnp.sum(whole.astype(F32) * moments, axis=0)
    grad_gate = (grad_hidden * u * s * (1.0 + g * (1.0 - s))).astype(BF16)
    grad_up = (grad_hidden * g * s).astype(BF16)
    return grad_gate, grad_up, lax.psum_scatter(sums, ("tp", "seq"), scatter_dimension=0, tiled=True)


def solution(mesh):
    tp = mesh.shape["tp"]
    per_device = by_ring if tp == 8 and mesh.shape["seq"] == 2 else by_gather
    rows = P(("rep", "seq"), "tp")
    return jax.shard_map(
        per_device,
        mesh=mesh,
        in_specs=(rows, rows, P("tp", None), P("tp"), rows),
        out_specs=(rows, rows, P(("rep", "tp", "seq"))),
        check_vma=False,
    )
```
